32 devices in a mesh: grp: 2 (over y), exp: 4 (over z), tp: 2 (over x), rep: 2 (over core).
Axes of the slice: x: 2, y: 2, z: 4, core: 2. Of those that a mesh axis runs over, the one named last changes fastest.
Arguments:
- tokens: bfloat16 [4096, 3584], P(('grp', 'exp', 'tp', 'rep')), parts along dimension 0, may hold values from -10 to 10
- routing: int32 [4096, 8], P(('grp', 'exp', 'tp', 'rep')), parts along dimension 0, may hold values from 0 to 255, as said below
- chosen: int32 [16], P('grp'), parts along dimension 0, may hold values from 0 to 3, as said below
- gate_matrix: bfloat16 [4, 3584, 1024], P('exp', None, 'tp'), may hold values from -0.09375 to 0.09375
- up_matrix: bfloat16 [4, 3584, 1024], P('exp', None, 'tp'), may hold values from -0.09375 to 0.09375
Outputs:
- hessians: float32 [16, 1024, 1024], P('grp', ('exp', 'rep'), 'tp'), parts along dimension 0
The draws below stay inside these ranges and needn't reach their ends.
There are 2 independent parts, one for each index of `grp`. The reference program is written for one: setup_inputs(seed, part) draws one part's arguments, and reference() takes and returns one part's arrays. A program takes and returns all parts, laid end to end along the dimension named above; an argument that names none is the same for every part. Nothing has to cross between parts.
Inputs may be any that keep to these rules, and one draw needn't show every extreme that they name: `routing`: each row names 8 different experts, at most one of them below 4. Among the rows of one device, each expert below 4 is named by at least one and at most 6 rows; one expert below 4, the same for all devices of a group, is named by exactly 6 rows of every device. `chosen`: each expert below 4 appears exactly twice.
All inputs are finite; a program needn't handle non-finite values.
Results may differ from the reference program's by a relative error of at most 0.004.
Values may be sent and summed in bfloat16 or wider, within the bound.
A program may use at most 64 MiB of HBM per device.

```python
import math
import jax
import jax.numpy as jnp
from jax import lax

FEATURE_HALF = 3584
INTERMEDIATE_HALF = 1024
ROUTED_EXPERTS = 256
TOPK = 8
TOK_DEV = 128
ROW_CAPACITY = 6
HELD_EXPERTS = 4
TOKENS = 2048


def draw_tokens(key, part):
    key = jax.random.fold_in(key, 5)
    key_rows, key_cols, key_noise = jax.random.split(key, 3)
    col_scale = jnp.exp(jax.random.uniform(key_cols, (1, FEATURE_HALF), minval=math.log(0.2), maxval=math.log(2.0)))
    row_scale = jnp.exp(jax.random.uniform(key_rows, (TOKENS, 1), minval=math.log(0.8), maxval=math.log(1.25)))
    values = jnp.clip(jax.random.normal(key_noise, (TOKENS, FEATURE_HALF)), -4.0, 4.0)
    return (row_scale * col_scale * values).astype(jnp.bfloat16)


def shuffle_row(row_key):
    return jax.random.permutation(row_key, TOK_DEV)


def draw_routing(key, part):
    key = jax.random.fold_in(key, 3)
    popular_key, load_key, key_order, key_slot, key_rest = jax.random.split(key, 5)
    block_list = TOKENS // TOK_DEV
    popular_expert = jax.random.randint(popular_key, (), 0, HELD_EXPERTS)
    owner_indices = jnp.arange(HELD_EXPERTS, dtype=jnp.int32)
    expert_loads = jax.random.randint(load_key, (block_list, HELD_EXPERTS), 1, ROW_CAPACITY // 2 + 1)
    expert_loads = jnp.where(owner_indices[None, :] == popular_expert, ROW_CAPACITY, expert_loads)
    bounds = jnp.cumsum(expert_loads, axis=1)
    positions = jnp.arange(TOK_DEV, dtype=jnp.int32)
    expert_labels = jnp.sum((positions[None, :, None] >= bounds[:, None, :]).astype(jnp.int32), axis=2)
    orders = jax.vmap(shuffle_row)(jax.random.split(key_order, block_list))
    expert_labels = jnp.take_along_axis(expert_labels, orders, axis=1)
    selected_slot = jax.random.randint(key_slot, (block_list, TOK_DEV), 0, TOPK)
    remaining_span = ROUTED_EXPERTS - HELD_EXPERTS
    start_offset = jax.random.randint(key_rest, (block_list, TOK_DEV), 0, remaining_span)
    step_stride = remaining_span // TOPK
    slot_indices = jnp.arange(TOPK, dtype=jnp.int32)
    other_experts = HELD_EXPERTS + (start_offset[:, :, None] + slot_indices[None, None, :] * step_stride) % remaining_span
    local_match = (slot_indices[None, None, :] == selected_slot[:, :, None]) & (expert_labels[:, :, None] < HELD_EXPERTS)
    routed = jnp.where(local_match, expert_labels[:, :, None], other_experts)
    return routed.reshape(TOKENS, TOPK).astype(jnp.int32)


def draw_chosen(key, part):
    key = jax.random.fold_in(key, 7)
    first_key, second_key = jax.random.split(key, 2)
    first_order = jax.random.permutation(first_key, HELD_EXPERTS)
    second_order = jax.random.permutation(second_key, HELD_EXPERTS)
    return jnp.concatenate([first_order, second_order], axis=0).astype(jnp.int32)


def block_levels(stream_key, dims, pieces, least, largest):
    loudness, own = 1.0, jax.random.fold_in(stream_key, 6)
    for position, parts in pieces:
        steps = jnp.exp(jax.random.uniform(jax.random.fold_in(own, position), (parts,), jnp.float32, least / len(pieces), largest / len(pieces)))
        loudness = loudness * jnp.repeat(steps, dims[position] // parts).reshape([-1 if axis == position else 1 for axis in range(len(dims))])
    return loudness


def centred(rng, shape, spread, bound, shards=(), held_as=jnp.bfloat16):
    entries = spread * jax.random.normal(rng, shape, jnp.float32)
    if shards:
        entries = entries * block_levels(rng, shape, shards, -0.22, 0.18)
    return jnp.clip(entries, -bound, bound).astype(held_as)


def setup_inputs(seed: int = 0, part: int = 0) -> dict:
    streams_of = jax.random.split(jax.random.key(seed), 6)
    part_splits = jax.random.split(jax.random.fold_in(streams_of[5], part), 6)
    return {
        "tokens": draw_tokens(jax.random.fold_in(jax.random.fold_in(streams_of[5], part), 71), part),
        "routing": draw_routing(jax.random.fold_in(jax.random.fold_in(streams_of[5], part), 71), part),
        "chosen": draw_chosen(jax.random.fold_in(jax.random.fold_in(streams_of[5], part), 71), part),
        "gate_matrix": centred(streams_of[3], (HELD_EXPERTS, FEATURE_HALF, INTERMEDIATE_HALF), FEATURE_HALF ** -0.5, 0.09375, ((0, 4), (2, 2))),
        "up_matrix": centred(streams_of[4], (HELD_EXPERTS, FEATURE_HALF, INTERMEDIATE_HALF), FEATURE_HALF ** -0.5, 0.09375, ((0, 4), (2, 2))),
    }


def reference(tokens, routing, chosen, gate_matrix, up_matrix):
    owner_indices = jnp.arange(HELD_EXPERTS, dtype=jnp.int32)
    counts = jnp.sum((routing[:, :, None] == owner_indices[None, None, :]).astype(jnp.float32), axis=(0, 1))
    row_limit = ROW_CAPACITY * (TOKENS // TOK_DEV)
    padded = jnp.concatenate([tokens, jnp.zeros((1, FEATURE_HALF), jnp.bfloat16)], axis=0)

    def per_expert(expert):
        routed = jnp.any(routing == expert, axis=1)
        row_index = jnp.nonzero(routed, size=row_limit, fill_value=TOKENS)[0].astype(jnp.int32)
        expert_rows = jnp.take(padded, row_index, axis=0)
        gate_out = jnp.dot(expert_rows, gate_matrix[expert], preferred_element_type=jnp.float32)
        up_out = jnp.dot(expert_rows, up_matrix[expert], preferred_element_type=jnp.float32)
        activated = (jax.nn.silu(gate_out) * up_out).astype(jnp.bfloat16)
        hessian = jnp.dot(activated.T, activated, preferred_element_type=jnp.float32)
        return hessian * (2.0 / counts[expert])

    return lax.map(per_expert, chosen)
```

```python
import functools

import jax
import jax.numpy as jnp
from jax import lax
from jax.experimental import pallas as pl
from jax.experimental.pallas import tpu as pltpu
from jax.sharding import PartitionSpec as P

FEATURE_HALF = 3584
ROW_CAPACITY = 6
BLOCK = 16
LANES = 128
MESH = pl.DeviceIdType.MESH


def local(tokens, routing, chosen, gate_matrix, up_matrix):
    owners = lax.axis_size("exp")
    groups = lax.axis_size("tp")
    row_count = tokens.shape[0]
    slot_count = ROW_CAPACITY
    owner_indices = jnp.arange(owners, dtype=jnp.int32)
    member = jnp.sum(
        (routing[:, :, None] == owner_indices[None, None, :]).astype(jnp.int32), axis=1
    )
    local_counts = jnp.sum(member, axis=0).astype(jnp.float32)
    counts = lax.psum(local_counts, ("exp", "tp", "rep"))
    slot_rank = (jnp.cumsum(member, axis=0) - member).T
    slot_indices = jnp.arange(slot_count, dtype=jnp.int32)
    placing_mask = (slot_rank[:, None, :] == slot_indices[None, :, None]) & (
        member.T[:, None, :] > 0
    )
    picker = placing_mask.reshape(owners * slot_count, row_count).astype(jnp.bfloat16)
    packed = jnp.dot(picker, tokens, preferred_element_type=jnp.float32).astype(jnp.bfloat16)
    gate_local = gate_matrix[0]
    up_local = up_matrix[0]
    arrived = lax.all_to_all(
        packed.reshape(owners, slot_count, FEATURE_HALF),
        "exp",
        split_axis=0,
        concat_axis=0,
        tiled=True,
    )
    flat_rows = arrived.reshape(owners * slot_count, FEATURE_HALF)
    token_rows = lax.all_gather(flat_rows, "tp", axis=0, tiled=True)
    gate_out = jnp.dot(token_rows, gate_local, preferred_element_type=jnp.float32)
    up_out = jnp.dot(token_rows, up_local, preferred_element_type=jnp.float32)
    activated = (jax.nn.silu(gate_out) * up_out).astype(jnp.bfloat16)
    panel_width = activated.shape[1]
    full_width = panel_width * groups
    product = lax.dot_general(
        lax.all_gather(activated, "tp", axis=1, tiled=True),
        activated,
        (((0,), (0,)), ((), ())),
        preferred_element_type=jnp.float32,
    )
    hess_tile = product
    my_expert = lax.axis_index("exp")
    my_count = jnp.sum(jnp.where(owner_indices == my_expert, counts, 0.0))
    hess_tile = hess_tile * (2.0 / my_count)
    tile_rows = hess_tile.reshape(owners, full_width // owners, panel_width)
    summed = lax.psum_scatter(tile_rows, "rep", scatter_dimension=1, tiled=True)
    relocated = lax.all_to_all(summed, "exp", split_axis=0, concat_axis=0, tiled=True)
    return jnp.take(relocated, chosen, axis=0)


def gather_kernel(owners, tokens_hbm, routing_ref, gate_hbm, up_hbm, cols_ref, rows_ref, counts_ref,
                  tokens, gate, up, packed, arrived, half_mine, half_other,
                  load_sem, z_send, z_recv, x_send, x_recv, c_send, c_recv,
                  az_send, az_recv, ar_send, ar_recv, as_send, as_recv):
    slots = ROW_CAPACITY
    me, t, r = lax.axis_index("exp"), lax.axis_index("tp"), lax.axis_index("rep")
    steps = STEP_ORDER
    half = tokens.shape[1] // 2
    panel = gate.shape[1]

    loads = [
        pltpu.make_async_copy(tokens_hbm, tokens, load_sem.at[0]),
        pltpu.make_async_copy(gate_hbm.at[0], gate, load_sem.at[1]),
        pltpu.make_async_copy(up_hbm.at[0], up, load_sem.at[2]),
    ]
    for load in loads:
        load.start()

    barrier = pltpu.get_barrier_semaphore()
    peers = [{"exp": me ^ k, "tp": t, "rep": r} for k in steps]
    peers += [{"exp": me, "tp": 1 - t, "rep": r}, {"exp": me, "tp": t, "rep": 1 - r}]
    peers += [{"exp": me, "tp": 1 - t, "rep": 1 - r}]
    for peer in peers:
        pl.semaphore_signal(barrier, inc=1, device_id=peer, device_id_type=MESH)

    routing = routing_ref[...]
    count = routing.shape[1]
    named = jnp.concatenate(
        [jnp.sum((routing == j).astype(jnp.float32), axis=0, keepdims=True) for j in range(owners)]
        + [jnp.zeros((8 - owners, count), jnp.float32)],
        axis=0,
    )
    earlier = (
        lax.broadcasted_iota(jnp.int32, (count, count), 0) < lax.broadcasted_iota(jnp.int32, (count, count), 1)
    ).astype(jnp.float32).astype(jnp.bfloat16)
    rank = jnp.dot(named.astype(jnp.bfloat16), earlier, preferred_element_type=jnp.float32)
    local_counts = jnp.sum(named, axis=1, keepdims=True)
    place = lax.broadcasted_iota(jnp.int32, (BLOCK, count), 0).astype(jnp.float32)
    one = lax.broadcasted_iota(jnp.int32, (BLOCK, 1), 0)
    first, second = [], []
    count_rows = jnp.zeros((BLOCK, 1), jnp.float32)
    for j in range(owners):
        here = named[j : j + 1, :] > 0.5
        first.append(jnp.where(here & (rank[j : j + 1, :] == place) & (place < slots), 1.0, 0.0))
        second.append(
            jnp.where(here & (rank[j : j + 1, :] == place - slots) & (place < 2 * slots), 1.0, 0.0)
        )
        count_rows = count_rows + jnp.where(one == 2 * slots + j, local_counts[j : j + 1, :], 0.0)
    first = jnp.concatenate(first, axis=0).astype(jnp.bfloat16)
    second = jnp.concatenate(second, axis=0).astype(jnp.bfloat16)
    count_rows = jnp.concatenate([count_rows] * owners, axis=0)

    loads[0].wait()
    packed[...] = (
        jnp.dot(first, tokens[:, :half], preferred_element_type=jnp.float32)
        + jnp.dot(second, tokens[:, half:], preferred_element_type=jnp.float32)
        + count_rows
    ).astype(jnp.bfloat16).reshape(packed.shape)
    arrived[t, me] = packed[me]

    pl.semaphore_wait(barrier, len(peers))

    def to_owner(k):
        return pltpu.make_async_remote_copy(
            src_ref=packed.at[me ^ k], dst_ref=arrived.at[t, me],
            send_sem=z_send.at[k], recv_sem=z_recv.at[k],
            device_id={"exp": me ^ k, "tp": t, "rep": r}, device_id_type=MESH,
        )

    def to_panel(k):
        return pltpu.make_async_remote_copy(
            src_ref=arrived.at[t, me ^ k], dst_ref=arrived.at[t, me ^ k],
            send_sem=x_send.at[k], recv_sem=x_recv.at[k],
            device_id={"exp": me, "tp": 1 - t, "rep": r}, device_id_type=MESH,
        )

    for k in steps:
        to_owner(k).start()
    to_panel(0).start()
    for k in steps:
        to_owner(k).wait_recv()
        to_panel(k).start()
    loads[1].wait()
    loads[2].wait()
    for k in (0,) + steps:
        to_panel(k).wait_recv()

    half_mine[...] = jnp.zeros_like(half_mine)
    half_mine[0:owners, :] = jnp.sum(
        arrived[:, :, 2 * slots : 2 * slots + owners, : half_mine.shape[1]].astype(jnp.float32), axis=(0, 1)
    )
    count_copy = pltpu.make_async_remote_copy(
        src_ref=half_mine, dst_ref=half_other, send_sem=c_send, recv_sem=c_recv,
        device_id={"exp": me, "tp": t, "rep": 1 - r}, device_id_type=MESH,
    )
    count_copy.start()

    sources = arrived.shape[0] * arrived.shape[1]
    total = sources * BLOCK
    kept = sources * slots
    out_row = lax.broadcasted_iota(jnp.int32, (kept, total), 0)
    in_row = lax.broadcasted_iota(jnp.int32, (kept, total), 1)
    source = in_row // BLOCK
    slot = in_row - source * BLOCK
    keep = ((slot < slots) & (out_row == source * slots + slot)).astype(jnp.float32).astype(jnp.bfloat16)
    width = 256
    for n in range(panel // width):
        at = slice(n * width, (n + 1) * width)
        x = arrived[...].reshape(total, half)

        def both(w):
            low = jnp.dot(x, w[:half, at], preferred_element_type=jnp.float32)
            high = jnp.dot(x, w[half:, at], preferred_element_type=jnp.float32)
            return low + pltpu.roll(high, total - slots, 0)

        g = both(gate)
        u = both(up)
        a = ((g / (1.0 + jnp.exp(-g))) * u).astype(jnp.bfloat16)
        cols_ref[me, r, :, at] = jnp.dot(keep, a, preferred_element_type=jnp.float32).astype(jnp.bfloat16)

    def to_group(k):
        return pltpu.make_async_remote_copy(
            src_ref=cols_ref.at[me, r], dst_ref=cols_ref.at[me, r],
            send_sem=az_send.at[k], recv_sem=az_recv.at[k],
            device_id={"exp": me ^ k, "tp": t, "rep": r}, device_id_type=MESH,
        )

    def to_core(k):
        return pltpu.make_async_remote_copy(
            src_ref=cols_ref.at[me ^ k, r], dst_ref=cols_ref.at[me ^ k, r],
            send_sem=ar_send.at[k], recv_sem=ar_recv.at[k],
            device_id={"exp": me, "tp": t, "rep": 1 - r}, device_id_type=MESH,
        )

    rows_width = rows_ref.shape[3]
    per_panel = panel // rows_width
    in_panel = (me * 2) // per_panel
    offset = me * 2 - in_panel * per_panel

    def strip(core):
        return pl.ds(pl.multiple_of((offset + core) * rows_width, rows_width), rows_width)

    def to_rows(k, core, sender):
        return pltpu.make_async_remote_copy(
            src_ref=cols_ref.at[me ^ k, sender, :, strip(core)], dst_ref=rows_ref.at[me ^ k, sender],
            send_sem=as_send.at[k, core], recv_sem=as_recv.at[k, sender],
            device_id={"exp": me, "tp": 1 - t, "rep": core}, device_id_type=MESH,
        )

    def pass_on(k):
        to_core(k).start()

        @pl.when(t == in_panel)
        def _():
            to_rows(k, 0, r).start()
            to_rows(k, 1, r).start()

    for k in steps:
        to_group(k).start()
    pass_on(0)
    for k in steps:
        to_group(k).wait_recv()
        pass_on(k)
    for k in (0,) + steps:
        to_core(k).wait_recv()

    @pl.when(t == in_panel)
    def _():
        rows_ref[...] = cols_ref[:, :, :, strip(r)]
        for k in (0,) + steps:
            to_rows(k, 0, r).wait_send()
            to_rows(k, 1, r).wait_send()

    @pl.when(t != in_panel)
    def _():
        for k in (0,) + steps:
            to_rows(k, r, 0).wait_recv()
            to_rows(k, r, 1).wait_recv()

    count_copy.wait()
    counts_ref[...] = half_mine[...] + half_other[...]
    for k in steps:
        to_owner(k).wait_send()
        to_group(k).wait_send()
    for k in (0,) + steps:
        to_panel(k).wait_send()
        to_core(k).wait_send()


def hessian_kernel(chosen_ref, cols_ref, rows_ref, counts_ref, out_hbm, tiles, sems):
    copies = []
    for s in range(out_hbm.shape[0]):
        e = chosen_ref[s]
        c = cols_ref[e].reshape(-1, cols_ref.shape[3])
        w = rows_ref[e].reshape(-1, rows_ref.shape[3])
        h = lax.dot_general(w, c, (((0,), (0,)), ((), ())), preferred_element_type=jnp.float32)
        tiles[s] = h * (2.0 / counts_ref[pl.ds(e, 1), :])
        copy = pltpu.make_async_copy(tiles.at[s], out_hbm.at[s], sems.at[s])
        copy.start()
        copies.append(copy)
    for copy in copies:
        copy.wait()


STEP_ORDER = (2, 3, 1)


def fused(owners, groups, tokens, routing, chosen, gate_matrix, up_matrix):
    features, panel = gate_matrix.shape[1:]
    kept = owners * groups * ROW_CAPACITY
    rows_width = panel * groups // (owners * 2)
    vmem = pl.BlockSpec(memory_space=pltpu.VMEM)
    hbm = pl.BlockSpec(memory_space=pl.ANY)
    dma = pltpu.SemaphoreType.DMA
    cols, rows, counts = pl.pallas_call(
        functools.partial(gather_kernel, owners),
        out_shape=(
            jax.ShapeDtypeStruct((owners, 2, kept, panel), jnp.bfloat16),
            jax.ShapeDtypeStruct((owners, 2, kept, rows_width), jnp.bfloat16),
            jax.ShapeDtypeStruct((8, panel), jnp.float32),
        ),
        in_specs=[hbm, vmem, hbm, hbm],
        out_specs=(vmem, vmem, vmem),
        scratch_shapes=[
            pltpu.VMEM(tokens.shape, jnp.bfloat16),
            pltpu.VMEM((features, panel), jnp.bfloat16),
            pltpu.VMEM((features, panel), jnp.bfloat16),
            pltpu.VMEM((owners, BLOCK, features // 2), jnp.bfloat16),
            pltpu.VMEM((groups, owners, BLOCK, features // 2), jnp.bfloat16),
            pltpu.VMEM((8, panel), jnp.float32),
            pltpu.VMEM((8, panel), jnp.float32),
            dma((3,)),
            dma((owners,)), dma((owners,)), dma((owners,)), dma((owners,)),
            dma, dma,
            dma((owners,)), dma((owners,)), dma((owners,)), dma((owners,)),
            dma((owners, 2)), dma((owners, 2)),
        ],
        compiler_params=pltpu.CompilerParams(
            collective_id=0, has_side_effects=True, vmem_limit_bytes=40 * 1024 * 1024
        ),
    )(tokens, routing.T, gate_matrix, up_matrix)
    out = (chosen.shape[0], rows_width, panel)
    return pl.pallas_call(
        hessian_kernel,
        out_shape=jax.ShapeDtypeStruct(out, jnp.float32),
        in_specs=[pl.BlockSpec(memory_space=pltpu.SMEM), vmem, vmem, vmem],
        out_specs=hbm,
        scratch_shapes=[pltpu.VMEM(out, jnp.float32), dma((out[0],))],
        compiler_params=pltpu.CompilerParams(vmem_limit_bytes=24 * 1024 * 1024),
    )(chosen, cols, rows, counts)


def solution(mesh):
    owners, groups, cores = mesh.shape["exp"], mesh.shape["tp"], mesh.shape["rep"]
    small = owners == 4 and groups == 2 and cores == 2 and 2 * ROW_CAPACITY + owners <= BLOCK
    return jax.shard_map(
        functools.partial(fused, owners, groups) if small else local,
        mesh=mesh,
        in_specs=(
            P(("grp", "exp", "tp", "rep"), None),
            P(("grp", "exp", "tp", "rep"), None),
            P("grp"),
            P("exp", None, "tp"),
            P("exp", None, "tp"),
        ),
        out_specs=P("grp", ("exp", "rep"), "tp"),
        check_vma=False,
    )
```

```python
import functools

import jax
import jax.numpy as jnp
from jax import lax
from jax.experimental import pallas as pl
from jax.experimental.pallas import tpu as pltpu
from jax.sharding import PartitionSpec as P

FEATURE_HALF = 3584
ROW_CAPACITY = 6
BLOCK = 48
CHUNK = 512
WIDTH = 256
EARLY = 32
FAR = (2, 3)
STEPS = (2, 3, 1)
MESH = pl.DeviceIdType.MESH


def local(tokens, routing, chosen, gate_matrix, up_matrix):
    owners = lax.axis_size("exp")
    groups = lax.axis_size("tp")
    row_count = tokens.shape[0]
    slot_count = ROW_CAPACITY
    owner_indices = jnp.arange(owners, dtype=jnp.int32)
    member = jnp.sum(
        (routing[:, :, None] == owner_indices[None, None, :]).astype(jnp.int32), axis=1
    )
    local_counts = jnp.sum(member, axis=0).astype(jnp.float32)
    counts = lax.psum(local_counts, ("exp", "tp", "rep"))
    slot_rank = (jnp.cumsum(member, axis=0) - member).T
    slot_indices = jnp.arange(slot_count, dtype=jnp.int32)
    placing_mask = (slot_rank[:, None, :] == slot_indices[None, :, None]) & (
        member.T[:, None, :] > 0
    )
    picker = placing_mask.reshape(owners * slot_count, row_count).astype(jnp.bfloat16)
    packed = jnp.dot(picker, tokens, preferred_element_type=jnp.float32).astype(jnp.bfloat16)
    gate_local = gate_matrix[0]
    up_local = up_matrix[0]
    arrived = lax.all_to_all(
        packed.reshape(owners, slot_count, FEATURE_HALF),
        "exp",
        split_axis=0,
        concat_axis=0,
        tiled=True,
    )
    flat_rows = arrived.reshape(owners * slot_count, FEATURE_HALF)
    token_rows = lax.all_gather(flat_rows, "tp", axis=0, tiled=True)
    gate_out = jnp.dot(token_rows, gate_local, preferred_element_type=jnp.float32)
    up_out = jnp.dot(token_rows, up_local, preferred_element_type=jnp.float32)
    activated = (jax.nn.silu(gate_out) * up_out).astype(jnp.bfloat16)
    panel_width = activated.shape[1]
    full_width = panel_width * groups
    product = lax.dot_general(
        lax.all_gather(activated, "tp", axis=1, tiled=True),
        activated,
        (((0,), (0,)), ((), ())),
        preferred_element_type=jnp.float32,
    )
    hess_tile = product
    my_expert = lax.axis_index("exp")
    my_count = jnp.sum(jnp.where(owner_indices == my_expert, counts, 0.0))
    hess_tile = hess_tile * (2.0 / my_count)
    tile_rows = hess_tile.reshape(owners, full_width // owners, panel_width)
    summed = lax.psum_scatter(tile_rows, "rep", scatter_dimension=1, tiled=True)
    relocated = lax.all_to_all(summed, "exp", split_axis=0, concat_axis=0, tiled=True)
    return jnp.take(relocated, chosen, axis=0)


def bits(mask):
    return mask.astype(jnp.float32).astype(jnp.bfloat16)


def hessian_kernel(owners, tokens_hbm, routing_hbm, gate_hbm, up_hbm, hess_ref,
                   tokens, routing_ref, gate, up, packed, arrived, half_mine, half_other, cols, rows, chooser,
                   load_sem, z_send, z_recv, f_send, f_recv, d_send, d_recv, c_send, c_recv,
                   az_send, az_recv, ar_send, ar_recv, as_send, as_recv):
    slots = ROW_CAPACITY
    me, t, r = lax.axis_index("exp"), lax.axis_index("tp"), lax.axis_index("rep")
    count, features = tokens.shape
    chunks = features // CHUNK
    pieces = gate.shape[1] // WIDTH
    sources = arrived.shape[0] * owners
    kept = sources * slots

    def place(e, tp, rep):
        return {"exp": e, "tp": tp, "rep": rep}

    loads = [
        pltpu.make_async_copy(routing_hbm, routing_ref, load_sem.at[0]),
        pltpu.make_async_copy(tokens_hbm, tokens, load_sem.at[1]),
        pltpu.make_async_copy(gate_hbm.at[0], gate, load_sem.at[2]),
        pltpu.make_async_copy(up_hbm.at[0], up, load_sem.at[3]),
    ]
    for load in loads:
        load.start()

    barrier = pltpu.get_barrier_semaphore()
    peers = [place(me ^ k, t ^ x, r ^ c) for k in range(owners) for x in (0, 1) for c in (0, 1)][1:]
    for peer in peers:
        pl.semaphore_signal(barrier, inc=1, device_id=peer, device_id_type=MESH)

    loads[0].wait()
    routing = routing_ref[...]
    named = jnp.concatenate(
        [jnp.sum((routing == j).astype(jnp.float32), axis=0, keepdims=True) for j in range(owners)]
        + [jnp.zeros((8 - owners, count), jnp.float32)],
        axis=0,
    )
    earlier = bits(
        lax.broadcasted_iota(jnp.int32, (count, count), 0) < lax.broadcasted_iota(jnp.int32, (count, count), 1)
    )
    rank = jnp.dot(named.astype(jnp.bfloat16), earlier, preferred_element_type=jnp.float32)
    local_counts = jnp.sum(named, axis=1, keepdims=True)
    row = lax.broadcasted_iota(jnp.int32, (BLOCK, count), 0)
    row_chunk = row // slots
    row_slot = (row - row_chunk * slots).astype(jnp.float32)
    one = lax.broadcasted_iota(jnp.int32, (BLOCK, 1), 0)
    picker = []
    count_rows = jnp.zeros((BLOCK, 1), jnp.float32)
    for j in range(owners):
        here = (named[j : j + 1, :] > 0.5) & (rank[j : j + 1, :] == row_slot)
        picker.append(
            jnp.concatenate([jnp.where(here & (row_chunk == c), 1.0, 0.0) for c in range(chunks)], axis=1)
        )
        count_rows = count_rows + jnp.where(one == chunks * slots + j, local_counts[j : j + 1, :], 0.0)
    picker = jnp.concatenate(picker, axis=0).astype(jnp.bfloat16)
    count_rows = jnp.concatenate([count_rows] * owners, axis=0)

    loads[1].wait()
    stacked = jnp.concatenate([tokens[:, c * CHUNK : (c + 1) * CHUNK] for c in range(chunks)], axis=0)
    packed[...] = (
        jnp.dot(picker, stacked, preferred_element_type=jnp.float32) + count_rows
    ).astype(jnp.bfloat16).reshape(packed.shape)

    pl.semaphore_wait(barrier, len(peers))

    early, late = pl.ds(0, EARLY), pl.ds(EARLY, BLOCK - EARLY)

    def remote(src, dst, send, recv, to):
        return pltpu.make_async_remote_copy(
            src_ref=src, dst_ref=dst, send_sem=send, recv_sem=recv, device_id=to, device_id_type=MESH
        )

    def to_owner(k):
        return remote(packed.at[me ^ k, early], arrived.at[t, me, early], z_send.at[k], z_recv.at[k],
                      place(me ^ k, t, r))

    def forward(k):
        here = arrived.at[t, me ^ k, early]
        return remote(here, here, f_send.at[k], f_recv.at[k], place(me, 1 - t, r))

    def direct(k, x, whole):
        part = pl.ds(0, BLOCK) if whole else late
        return remote(packed.at[me ^ k, part], arrived.at[t, me, part], d_send.at[k, x], d_recv.at[k, x],
                      place(me ^ k, t ^ x, r))

    directs = [(0, 1, True), (1, 0, True), (1, 1, True)] + [(k, x, False) for k in FAR for x in (0, 1)]
    for k in FAR:
        to_owner(k).start()
    for d in directs:
        direct(*d).start()
    arrived[t, me] = packed[me]

    total = sources * BLOCK
    q = lax.broadcasted_iota(jnp.int32, (chunks * kept, 1), 0)
    q_chunk = q // kept
    q_row = q - q_chunk * kept
    q_source = q_row // slots
    target = q_source * BLOCK + q_chunk * slots + (q_row - q_source * slots)
    chooser[...] = bits(lax.broadcasted_iota(jnp.int32, (chunks * kept, total), 1) == target)

    for k in FAR:
        to_owner(k).wait_recv()
        forward(k).start()
    for d in directs:
        direct(*d).wait_recv()
    for k in FAR:
        forward(k).wait_recv()

    half_mine[...] = jnp.zeros_like(half_mine)
    half_mine[0:owners, :] = jnp.sum(
        arrived[:, :, chunks * slots : chunks * slots + owners, :].astype(jnp.float32), axis=(0, 1)
    )
    count_copy = remote(half_mine, half_other, c_send, c_recv, place(me, t, 1 - r))
    count_copy.start()

    chosen_rows = jnp.dot(
        chooser[...], arrived[...].reshape(total, CHUNK), preferred_element_type=jnp.float32
    ).astype(jnp.bfloat16)
    x = jnp.concatenate([chosen_rows[c * kept : (c + 1) * kept] for c in range(chunks)], axis=1)
    loads[2].wait()
    loads[3].wait()

    def to_group(k, n):
        here = cols.at[me, r, n]
        return remote(here, here, az_send.at[k, n], az_recv.at[k, n], place(me ^ k, t, r))

    def to_core(k, n):
        here = cols.at[me ^ k, r, n]
        return remote(here, here, ar_send.at[k, n], ar_recv.at[k, n], place(me, t, 1 - r))

    strip_width = rows.shape[3]

    def strip(core):
        return pl.ds(pl.multiple_of(core * strip_width, strip_width), strip_width)

    def to_strip(n, core):
        return remote(cols.at[me, r, n, :, strip(core)], rows.at[me, r], as_send.at[n, core], as_recv.at[me, r],
                      place(t * pieces + n, 1 - t, core))

    def strip_arrival(e, core):
        return remote(rows.at[e, core], rows.at[e, core], as_send.at[0, 0], as_recv.at[e, core], place(me, 1 - t, r))

    for n in range(pieces):
        at = slice(n * WIDTH, (n + 1) * WIDTH)
        g = jnp.dot(x, gate[:, at], preferred_element_type=jnp.float32)
        u = jnp.dot(x, up[:, at], preferred_element_type=jnp.float32)
        cols[me, r, n] = ((g / (1.0 + jnp.exp(-g))) * u).astype(jnp.bfloat16)
        for k in STEPS:
            to_group(k, n).start()
        for core in (0, 1):
            to_strip(n, core).start()
        to_core(0, n).start()

    count_copy.wait()
    half_mine[...] = 2.0 / jnp.maximum(half_mine[...] + half_other[...], 1.0)

    in_panel = me // pieces

    def hessian(k):
        e = me ^ k
        for n in range(pieces):
            to_core(k, n).wait_recv()

        @pl.when(t == in_panel)
        def _():
            rows[e] = cols[e, :, me - in_panel * pieces, :, strip(r)]

        @pl.when(t != in_panel)
        def _():
            for core in (0, 1):
                strip_arrival(e, core).wait_recv()

        left = rows[e].reshape(2 * kept, strip_width)
        scale = half_mine[pl.ds(e, 1), :]
        for n in range(pieces):
            right = jnp.concatenate([cols[e, 0, n], cols[e, 1, n]], axis=0)
            h = lax.dot_general(left, right, (((0,), (0,)), ((), ())), preferred_element_type=jnp.float32)
            at = slice(n * WIDTH, (n + 1) * WIDTH)
            hess_ref[e, :, at] = h * scale[:, at]

    for n in range(pieces):
        for k in (1,) + FAR:
            if n == pieces - 1 and k == FAR[0]:
                hessian(0)
            to_group(k, n).wait_recv()
            to_core(k, n).start()
    for k in (1,) + FAR:
        hessian(k)

    for k in FAR:
        to_owner(k).wait_send()
        forward(k).wait_send()
    for d in directs:
        direct(*d).wait_send()
    for n in range(pieces):
        for k in STEPS:
            to_group(k, n).wait_send()
        for k in (0,) + STEPS:
            to_core(k, n).wait_send()
        for core in (0, 1):
            to_strip(n, core).wait_send()


def order_kernel(chosen_ref, hess_ref, out_hbm, sems):
    copies = [
        pltpu.make_async_copy(hess_ref.at[chosen_ref[s]], out_hbm.at[s], sems.at[s]) for s in range(out_hbm.shape[0])
    ]
    for copy in copies:
        copy.start()
    for copy in copies:
        copy.wait()


def fused(owners, groups, tokens, routing, chosen, gate_matrix, up_matrix):
    features, panel = gate_matrix.shape[1:]
    kept = owners * groups * ROW_CAPACITY
    chunks, pieces = features // CHUNK, panel // WIDTH
    rows_width = panel * groups // (owners * 2)
    vmem = pl.BlockSpec(memory_space=pltpu.VMEM)
    hbm = pl.BlockSpec(memory_space=pltpu.HBM)
    dma = pltpu.SemaphoreType.DMA
    hess = pl.pallas_call(
        functools.partial(hessian_kernel, owners),
        out_shape=jax.ShapeDtypeStruct((owners, rows_width, panel), jnp.float32),
        in_specs=[hbm, hbm, hbm, hbm],
        out_specs=vmem,
        scratch_shapes=[
            pltpu.VMEM(tokens.shape, jnp.bfloat16),
            pltpu.VMEM(routing.shape[::-1], jnp.int32),
            pltpu.VMEM((features, panel), jnp.bfloat16),
            pltpu.VMEM((features, panel), jnp.bfloat16),
            pltpu.VMEM((owners, BLOCK, CHUNK), jnp.bfloat16),
            pltpu.VMEM((groups, owners, BLOCK, CHUNK), jnp.bfloat16),
            pltpu.VMEM((8, panel), jnp.float32),
            pltpu.VMEM((8, panel), jnp.float32),
            pltpu.VMEM((owners, 2, pieces, kept, WIDTH), jnp.bfloat16),
            pltpu.VMEM((owners, 2, kept, rows_width), jnp.bfloat16),
            pltpu.VMEM((chunks * kept, owners * groups * BLOCK), jnp.bfloat16),
            dma((4,)),
            dma((owners,)), dma((owners,)), dma((owners,)), dma((owners,)),
            dma((owners, 2)), dma((owners, 2)),
            dma, dma,
            dma((owners, pieces)), dma((owners, pieces)), dma((owners, pieces)), dma((owners, pieces)),
            dma((pieces, 2)), dma((owners, 2)),
        ],
        compiler_params=pltpu.CompilerParams(
            collective_id=0, has_side_effects=True, vmem_limit_bytes=48 * 1024 * 1024
        ),
    )(*[pltpu.with_memory_space_constraint(a, pltpu.HBM) for a in (tokens, routing.T, gate_matrix, up_matrix)])
    out = (chosen.shape[0], rows_width, panel)
    return pl.pallas_call(
        order_kernel,
        out_shape=jax.ShapeDtypeStruct(out, jnp.float32),
        in_specs=[pl.BlockSpec(memory_space=pltpu.SMEM), vmem],
        out_specs=hbm,
        scratch_shapes=[dma((out[0],))],
        compiler_params=pltpu.CompilerParams(vmem_limit_bytes=24 * 1024 * 1024),
    )(chosen, hess)


def solution(mesh):
    owners, groups, cores = mesh.shape["exp"], mesh.shape["tp"], mesh.shape["rep"]
    small = owners == 4 and groups == 2 and cores == 2
    return jax.shard_map(
        functools.partial(fused, owners, groups) if small else local,
        mesh=mesh,
        in_specs=(
            P(("grp", "exp", "tp", "rep"), None),
            P(("grp", "exp", "tp", "rep"), None),
            P("grp"),
            P("exp", None, "tp"),
            P("exp", None, "tp"),
        ),
        out_specs=P("grp", ("exp", "rep"), "tp"),
        check_vma=False,
    )
```

```python
import functools

import jax
import jax.numpy as jnp
from jax import lax
from jax.experimental import pallas as pl
from jax.experimental.pallas import tpu as pltpu
from jax.sharding import PartitionSpec as P

FEATURE_HALF = 3584
ROW_CAPACITY = 6
BLOCK = 48
CHUNK = 512
WIDTH = 256
EARLY = 32
FAR = (2, 3)
STEPS = (2, 3, 1)
MESH = pl.DeviceIdType.MESH


def local(tokens, routing, chosen, gate_matrix, up_matrix):
    owners = lax.axis_size("exp")
    groups = lax.axis_size("tp")
    row_count = tokens.shape[0]
    slot_count = ROW_CAPACITY
    owner_indices = jnp.arange(owners, dtype=jnp.int32)
    member = jnp.sum(
        (routing[:, :, None] == owner_indices[None, None, :]).astype(jnp.int32), axis=1
    )
    local_counts = jnp.sum(member, axis=0).astype(jnp.float32)
    counts = lax.psum(local_counts, ("exp", "tp", "rep"))
    slot_rank = (jnp.cumsum(member, axis=0) - member).T
    slot_indices = jnp.arange(slot_count, dtype=jnp.int32)
    placing_mask = (slot_rank[:, None, :] == slot_indices[None, :, None]) & (
        member.T[:, None, :] > 0
    )
    picker = placing_mask.reshape(owners * slot_count, row_count).astype(jnp.bfloat16)
    packed = jnp.dot(picker, tokens, preferred_element_type=jnp.float32).astype(jnp.bfloat16)
    gate_local = gate_matrix[0]
    up_local = up_matrix[0]
    arrived = lax.all_to_all(
        packed.reshape(owners, slot_count, FEATURE_HALF),
        "exp",
        split_axis=0,
        concat_axis=0,
        tiled=True,
    )
    flat_rows = arrived.reshape(owners * slot_count, FEATURE_HALF)
    token_rows = lax.all_gather(flat_rows, "tp", axis=0, tiled=True)
    gate_out = jnp.dot(token_rows, gate_local, preferred_element_type=jnp.float32)
    up_out = jnp.dot(token_rows, up_local, preferred_element_type=jnp.float32)
    activated = (jax.nn.silu(gate_out) * up_out).astype(jnp.bfloat16)
    panel_width = activated.shape[1]
    full_width = panel_width * groups
    product = lax.dot_general(
        lax.all_gather(activated, "tp", axis=1, tiled=True),
        activated,
        (((0,), (0,)), ((), ())),
        preferred_element_type=jnp.float32,
    )
    hess_tile = product
    my_expert = lax.axis_index("exp")
    my_count = jnp.sum(jnp.where(owner_indices == my_expert, counts, 0.0))
    hess_tile = hess_tile * (2.0 / my_count)
    tile_rows = hess_tile.reshape(owners, full_width // owners, panel_width)
    summed = lax.psum_scatter(tile_rows, "rep", scatter_dimension=1, tiled=True)
    relocated = lax.all_to_all(summed, "exp", split_axis=0, concat_axis=0, tiled=True)
    return jnp.take(relocated, chosen, axis=0)


def bits(mask):
    return mask.astype(jnp.float32).astype(jnp.bfloat16)


def hessian_kernel(owners, tokens_hbm, routing_hbm, gate_hbm, up_hbm, hess_ref,
                   tokens, routing_ref, gate, up, packed, arrived, half_mine, half_other, cols, rows, chooser,
                   load_sem, z_send, z_recv, f_send, f_recv, d_send, d_recv, c_send, c_recv,
                   az_send, az_recv, ar_send, ar_recv, as_send, as_recv):
    slots = ROW_CAPACITY
    me, t, r = lax.axis_index("exp"), lax.axis_index("tp"), lax.axis_index("rep")
    count, features = tokens.shape
    chunks = features // CHUNK
    pieces = gate.shape[1] // WIDTH
    sources = arrived.shape[0] * owners
    kept = sources * slots

    def place(e, tp, rep):
        return {"exp": e, "tp": tp, "rep": rep}

    barrier = pltpu.get_barrier_semaphore()
    peers = [place(me ^ k, t ^ x, r ^ c) for k in (3, 2, 1) for x, c in ((0, 0), (1, 0), (1, 1))]
    peers += [place(me, t ^ x, r ^ c) for x, c in ((1, 0), (1, 1), (0, 1))]
    for peer in peers:
        pl.semaphore_signal(barrier, inc=1, device_id=peer, device_id_type=MESH)

    loads = [
        pltpu.make_async_copy(routing_hbm, routing_ref, load_sem.at[0]),
        pltpu.make_async_copy(tokens_hbm, tokens, load_sem.at[1]),
        pltpu.make_async_copy(gate_hbm.at[0], gate, load_sem.at[2]),
        pltpu.make_async_copy(up_hbm.at[0], up, load_sem.at[3]),
    ]
    for load in loads:
        load.start()

    loads[0].wait()
    routing = routing_ref[...]
    named = jnp.concatenate(
        [jnp.sum((routing == j).astype(jnp.float32), axis=0, keepdims=True) for j in range(owners)]
        + [jnp.zeros((8 - owners, count), jnp.float32)],
        axis=0,
    )
    earlier = bits(
        lax.broadcasted_iota(jnp.int32, (count, count), 0) < lax.broadcasted_iota(jnp.int32, (count, count), 1)
    )
    rank = jnp.dot(named.astype(jnp.bfloat16), earlier, preferred_element_type=jnp.float32)
    local_counts = jnp.sum(named, axis=1, keepdims=True)
    row = lax.broadcasted_iota(jnp.int32, (BLOCK, count), 0)
    row_chunk = row // slots
    row_slot = (row - row_chunk * slots).astype(jnp.float32)
    one = lax.broadcasted_iota(jnp.int32, (BLOCK, 1), 0)
    picker = []
    count_rows = jnp.zeros((BLOCK, 1), jnp.float32)
    for j in range(owners):
        here = (named[j : j + 1, :] > 0.5) & (rank[j : j + 1, :] == row_slot)
        picker.append(
            jnp.concatenate([jnp.where(here & (row_chunk == c), 1.0, 0.0) for c in range(chunks)], axis=1)
        )
        count_rows = count_rows + jnp.where(one == chunks * slots + j, local_counts[j : j + 1, :], 0.0)
    picker = jnp.concatenate(picker, axis=0).astype(jnp.bfloat16)
    count_rows = jnp.concatenate([count_rows] * owners, axis=0)

    loads[1].wait()
    stacked = jnp.concatenate([tokens[:, c * CHUNK : (c + 1) * CHUNK] for c in range(chunks)], axis=0)
    packed[...] = (
        jnp.dot(picker, stacked, preferred_element_type=jnp.float32) + count_rows
    ).astype(jnp.bfloat16).reshape(packed.shape)

    pl.semaphore_wait(barrier, len(peers))

    early, late = pl.ds(0, EARLY), pl.ds(EARLY, BLOCK - EARLY)

    def remote(src, dst, send, recv, to):
        return pltpu.make_async_remote_copy(
            src_ref=src, dst_ref=dst, send_sem=send, recv_sem=recv, device_id=to, device_id_type=MESH
        )

    def to_owner(k):
        return remote(packed.at[me ^ k, early], arrived.at[t, me, early], z_send.at[k], z_recv.at[k],
                      place(me ^ k, t, r))

    def forward(k):
        here = arrived.at[t, me ^ k, early]
        return remote(here, here, f_send.at[k], f_recv.at[k], place(me, 1 - t, r))

    def direct(k, x, whole):
        part = pl.ds(0, BLOCK) if whole else late
        return remote(packed.at[me ^ k, part], arrived.at[t, me, part], d_send.at[k, x], d_recv.at[k, x],
                      place(me ^ k, t ^ x, r))

    directs = [(0, 1, True), (1, 0, True), (1, 1, True)] + [(k, x, False) for k in FAR for x in (0, 1)]
    for k in FAR:
        to_owner(k).start()
    for d in directs:
        direct(*d).start()
    arrived[t, me] = packed[me]

    total = sources * BLOCK
    q = lax.broadcasted_iota(jnp.int32, (chunks * kept, 1), 0)
    q_chunk = q // kept
    q_row = q - q_chunk * kept
    q_source = q_row // slots
    target = q_source * BLOCK + q_chunk * slots + (q_row - q_source * slots)
    chooser[...] = bits(lax.broadcasted_iota(jnp.int32, (chunks * kept, total), 1) == target)

    for k in FAR:
        to_owner(k).wait_recv()
        forward(k).start()
    for d in directs:
        direct(*d).wait_recv()
    for k in FAR:
        forward(k).wait_recv()

    half_mine[...] = jnp.zeros_like(half_mine)
    half_mine[0:owners, :] = jnp.sum(
        arrived[:, :, chunks * slots : chunks * slots + owners, :].astype(jnp.float32), axis=(0, 1)
    )
    count_copy = remote(half_mine, half_other, c_send, c_recv, place(me, t, 1 - r))
    count_copy.start()

    chosen_rows = jnp.dot(
        chooser[...], arrived[...].reshape(total, CHUNK), preferred_element_type=jnp.float32
    ).astype(jnp.bfloat16)
    x = jnp.concatenate([chosen_rows[c * kept : (c + 1) * kept] for c in range(chunks)], axis=1)
    loads[2].wait()
    loads[3].wait()

    def to_group(k, n):
        here = cols.at[me, r, n]
        return remote(here, here, az_send.at[k, n], az_recv.at[k, n], place(me ^ k, t, r))

    def to_core(k, n):
        here = cols.at[me ^ k, r, n]
        return remote(here, here, ar_send.at[k, n], ar_recv.at[k, n], place(me, t, 1 - r))

    strip_width = rows.shape[3]

    def strip(core):
        return pl.ds(pl.multiple_of(core * strip_width, strip_width), strip_width)

    def to_strip(n, core):
        return remote(cols.at[me, r, n, :, strip(core)], rows.at[me, r], as_send.at[n, core], as_recv.at[me, r],
                      place(t * pieces + n, 1 - t, core))

    def strip_arrival(e, core):
        return remote(rows.at[e, core], rows.at[e, core], as_send.at[0, 0], as_recv.at[e, core], place(me, 1 - t, r))

    for n in range(pieces):
        at = slice(n * WIDTH, (n + 1) * WIDTH)
        g = jnp.dot(x, gate[:, at], preferred_element_type=jnp.float32)
        u = jnp.dot(x, up[:, at], preferred_element_type=jnp.float32)
        cols[me, r, n] = ((g / (1.0 + jnp.exp(-g))) * u).astype(jnp.bfloat16)
        for k in STEPS:
            to_group(k, n).start()
        to_core(0, n).start()

    for n in range(pieces):
        for core in (0, 1):
            to_strip(n, core).start()
    count_copy.wait()
    half_mine[...] = 2.0 / jnp.maximum(half_mine[...] + half_other[...], 1.0)

    in_panel = me // pieces

    def hessian(k):
        e = me ^ k
        for n in range(pieces):
            to_core(k, n).wait_recv()

        @pl.when(t == in_panel)
        def _():
            rows[e] = cols[e, :, me - in_panel * pieces, :, strip(r)]

        @pl.when(t != in_panel)
        def _():
            for core in (0, 1):
                strip_arrival(e, core).wait_recv()

        left = rows[e].reshape(2 * kept, strip_width)
        scale = half_mine[pl.ds(e, 1), :]
        for n in range(pieces):
            right = jnp.concatenate([cols[e, 0, n], cols[e, 1, n]], axis=0)
            h = lax.dot_general(left, right, (((0,), (0,)), ((), ())), preferred_element_type=jnp.float32)
            at = slice(n * WIDTH, (n + 1) * WIDTH)
            hess_ref[e, :, at] = h * scale[:, at]

    for n in range(pieces):
        for k in (1,) + FAR:
            if n == pieces - 1 and k == FAR[0]:
                hessian(0)
            to_group(k, n).wait_recv()
            to_core(k, n).start()
    for k in (1,) + FAR:
        hessian(k)

    for k in FAR:
        to_owner(k).wait_send()
        forward(k).wait_send()
    for d in directs:
        direct(*d).wait_send()
    for n in range(pieces):
        for k in STEPS:
            to_group(k, n).wait_send()
        for k in (0,) + STEPS:
            to_core(k, n).wait_send()
        for core in (0, 1):
            to_strip(n, core).wait_send()


def order_kernel(chosen_ref, hess_ref, out_hbm, sems):
    copies = [
        pltpu.make_async_copy(hess_ref.at[chosen_ref[s]], out_hbm.at[s], sems.at[s]) for s in range(out_hbm.shape[0])
    ]
    for copy in copies:
        copy.start()
    for copy in copies:
        copy.wait()


def fused(owners, groups, tokens, routing, chosen, gate_matrix, up_matrix):
    features, panel = gate_matrix.shape[1:]
    kept = owners * groups * ROW_CAPACITY
    chunks, pieces = features // CHUNK, panel // WIDTH
    rows_width = panel * groups // (owners * 2)
    vmem = pl.BlockSpec(memory_space=pltpu.VMEM)
    hbm = pl.BlockSpec(memory_space=pltpu.HBM)
    dma = pltpu.SemaphoreType.DMA
    hess = pl.pallas_call(
        functools.partial(hessian_kernel, owners),
        out_shape=jax.ShapeDtypeStruct((owners, rows_width, panel), jnp.float32),
        in_specs=[hbm, hbm, hbm, hbm],
        out_specs=vmem,
        scratch_shapes=[
            pltpu.VMEM(tokens.shape, jnp.bfloat16),
            pltpu.VMEM(routing.shape[::-1], jnp.int32),
            pltpu.VMEM((features, panel), jnp.bfloat16),
            pltpu.VMEM((features, panel), jnp.bfloat16),
            pltpu.VMEM((owners, BLOCK, CHUNK), jnp.bfloat16),
            pltpu.VMEM((groups, owners, BLOCK, CHUNK), jnp.bfloat16),
            pltpu.VMEM((8, panel), jnp.float32),
            pltpu.VMEM((8, panel), jnp.float32),
            pltpu.VMEM((owners, 2, pieces, kept, WIDTH), jnp.bfloat16),
            pltpu.VMEM((owners, 2, kept, rows_width), jnp.bfloat16),
            pltpu.VMEM((chunks * kept, owners * groups * BLOCK), jnp.bfloat16),
            dma((4,)),
            dma((owners,)), dma((owners,)), dma((owners,)), dma((owners,)),
            dma((owners, 2)), dma((owners, 2)),
            dma, dma,
            dma((owners, pieces)), dma((owners, pieces)), dma((owners, pieces)), dma((owners, pieces)),
            dma((pieces, 2)), dma((owners, 2)),
        ],
        compiler_params=pltpu.CompilerParams(
            collective_id=0, has_side_effects=True, vmem_limit_bytes=48 * 1024 * 1024
        ),
    )(*[pltpu.with_memory_space_constraint(a, pltpu.HBM) for a in (tokens, routing.T, gate_matrix, up_matrix)])
    out = (chosen.shape[0], rows_width, panel)
    return pl.pallas_call(
        order_kernel,
        out_shape=jax.ShapeDtypeStruct(out, jnp.float32),
        in_specs=[pl.BlockSpec(memory_space=pltpu.SMEM), vmem],
        out_specs=hbm,
        scratch_shapes=[dma((out[0],))],
        compiler_params=pltpu.CompilerParams(vmem_limit_bytes=24 * 1024 * 1024),
    )(chosen, hess)


def solution(mesh):
    owners, groups, cores = mesh.shape["exp"], mesh.shape["tp"], mesh.shape["rep"]
    small = owners == 4 and groups == 2 and cores == 2
    return jax.shard_map(
        functools.partial(fused, owners, groups) if small else local,
        mesh=mesh,
        in_specs=(
            P(("grp", "exp", "tp", "rep"), None),
            P(("grp", "exp", "tp", "rep"), None),
            P("grp"),
            P("exp", None, "tp"),
            P("exp", None, "tp"),
        ),
        out_specs=P("grp", ("exp", "rep"), "tp"),
        check_vma=False,
    )
```

```python
import functools

import jax
import jax.numpy as jnp
from jax import lax
from jax.experimental import pallas as pl
from jax.experimental.pallas import tpu as pltpu
from jax.sharding import PartitionSpec as P

FEATURE_HALF = 3584
ROW_CAPACITY = 6
BLOCK = 48
CHUNK = 512
WIDTH = 256
EARLY = 32
FAR = (2, 3)
STEPS = (2, 3, 1)
MESH = pl.DeviceIdType.MESH


def local(tokens, routing, chosen, gate_matrix, up_matrix):
    owners = lax.axis_size("exp")
    groups = lax.axis_size("tp")
    row_count = tokens.shape[0]
    slot_count = ROW_CAPACITY
    owner_indices = jnp.arange(owners, dtype=jnp.int32)
    member = jnp.sum(
        (routing[:, :, None] == owner_indices[None, None, :]).astype(jnp.int32), axis=1
    )
    local_counts = jnp.sum(member, axis=0).astype(jnp.float32)
    counts = lax.psum(local_counts, ("exp", "tp", "rep"))
    slot_rank = (jnp.cumsum(member, axis=0) - member).T
    slot_indices = jnp.arange(slot_count, dtype=jnp.int32)
    placing_mask = (slot_rank[:, None, :] == slot_indices[None, :, None]) & (
        member.T[:, None, :] > 0
    )
    picker = placing_mask.reshape(owners * slot_count, row_count).astype(jnp.bfloat16)
    packed = jnp.dot(picker, tokens, preferred_element_type=jnp.float32).astype(jnp.bfloat16)
    gate_local = gate_matrix[0]
    up_local = up_matrix[0]
    arrived = lax.all_to_all(
        packed.reshape(owners, slot_count, FEATURE_HALF),
        "exp",
        split_axis=0,
        concat_axis=0,
        tiled=True,
    )
    flat_rows = arrived.reshape(owners * slot_count, FEATURE_HALF)
    token_rows = lax.all_gather(flat_rows, "tp", axis=0, tiled=True)
    gate_out = jnp.dot(token_rows, gate_local, preferred_element_type=jnp.float32)
    up_out = jnp.dot(token_rows, up_local, preferred_element_type=jnp.float32)
    activated = (jax.nn.silu(gate_out) * up_out).astype(jnp.bfloat16)
    panel_width = activated.shape[1]
    full_width = panel_width * groups
    product = lax.dot_general(
        lax.all_gather(activated, "tp", axis=1, tiled=True),
        activated,
        (((0,), (0,)), ((), ())),
        preferred_element_type=jnp.float32,
    )
    hess_tile = product
    my_expert = lax.axis_index("exp")
    my_count = jnp.sum(jnp.where(owner_indices == my_expert, counts, 0.0))
    hess_tile = hess_tile * (2.0 / my_count)
    tile_rows = hess_tile.reshape(owners, full_width // owners, panel_width)
    summed = lax.psum_scatter(tile_rows, "rep", scatter_dimension=1, tiled=True)
    relocated = lax.all_to_all(summed, "exp", split_axis=0, concat_axis=0, tiled=True)
    return jnp.take(relocated, chosen, axis=0)


def bits(mask):
    return mask.astype(jnp.float32).astype(jnp.bfloat16)


def hessian_kernel(owners, tokens_hbm, routing_hbm, gate_hbm, up_hbm, hess_ref,
                   tokens, routing_ref, gate, up, packed, arrived, half_mine, half_other, cols, rows, chooser,
                   load_sem, z_send, z_recv, f_send, f_recv, d_send, d_recv, c_send, c_recv,
                   az_send, az_recv, ar_send, ar_recv, as_send, as_recv):
    slots = ROW_CAPACITY
    me, t, r = lax.axis_index("exp"), lax.axis_index("tp"), lax.axis_index("rep")
    count, features = tokens.shape
    chunks = features // CHUNK
    pieces = gate.shape[1] // WIDTH
    sources = arrived.shape[0] * owners
    kept = sources * slots

    def place(e, tp, rep):
        return {"exp": e, "tp": tp, "rep": rep}

    barrier = pltpu.get_barrier_semaphore()
    peers = [place(me ^ k, t ^ x, r ^ c) for k in (3, 2, 1) for x, c in ((0, 0), (1, 0), (1, 1))]
    peers += [place(me, t ^ x, r ^ c) for x, c in ((1, 0), (1, 1), (0, 1))]
    for peer in peers:
        pl.semaphore_signal(barrier, inc=1, device_id=peer, device_id_type=MESH)

    loads = [
        pltpu.make_async_copy(routing_hbm, routing_ref, load_sem.at[0]),
        pltpu.make_async_copy(tokens_hbm, tokens, load_sem.at[1]),
        pltpu.make_async_copy(gate_hbm.at[0], gate, load_sem.at[2]),
        pltpu.make_async_copy(up_hbm.at[0], up, load_sem.at[3]),
    ]
    for load in loads:
        load.start()

    loads[0].wait()
    routing = routing_ref[...]
    named = jnp.concatenate(
        [jnp.sum((routing == j).astype(jnp.float32), axis=0, keepdims=True) for j in range(owners)]
        + [jnp.zeros((8 - owners, count), jnp.float32)],
        axis=0,
    )
    earlier = bits(
        lax.broadcasted_iota(jnp.int32, (count, count), 0) < lax.broadcasted_iota(jnp.int32, (count, count), 1)
    )
    rank = jnp.dot(named.astype(jnp.bfloat16), earlier, preferred_element_type=jnp.float32)
    local_counts = jnp.sum(named, axis=1, keepdims=True)
    row = lax.broadcasted_iota(jnp.int32, (BLOCK, count), 0)
    row_chunk = row // slots
    row_slot = (row - row_chunk * slots).astype(jnp.float32)
    one = lax.broadcasted_iota(jnp.int32, (BLOCK, 1), 0)
    picker = []
    count_rows = jnp.zeros((BLOCK, 1), jnp.float32)
    for j in range(owners):
        here = (named[j : j + 1, :] > 0.5) & (rank[j : j + 1, :] == row_slot)
        picker.append(
            jnp.concatenate([jnp.where(here & (row_chunk == c), 1.0, 0.0) for c in range(chunks)], axis=1)
        )
        count_rows = count_rows + jnp.where(one == chunks * slots + j, local_counts[j : j + 1, :], 0.0)
    picker = jnp.concatenate(picker, axis=0).astype(jnp.bfloat16)
    count_rows = jnp.concatenate([count_rows] * owners, axis=0)

    loads[1].wait()
    stacked = jnp.concatenate([tokens[:, c * CHUNK : (c + 1) * CHUNK] for c in range(chunks)], axis=0)
    packed[...] = (
        jnp.dot(picker, stacked, preferred_element_type=jnp.float32) + count_rows
    ).astype(jnp.bfloat16).reshape(packed.shape)

    pl.semaphore_wait(barrier, len(peers))

    early, late = pl.ds(0, EARLY), pl.ds(EARLY, BLOCK - EARLY)

    def remote(src, dst, send, recv, to):
        return pltpu.make_async_remote_copy(
            src_ref=src, dst_ref=dst, send_sem=send, recv_sem=recv, device_id=to, device_id_type=MESH
        )

    def to_owner(k):
        return remote(packed.at[me ^ k, early], arrived.at[t, me, early], z_send.at[k], z_recv.at[k],
                      place(me ^ k, t, r))

    def forward(k):
        here = arrived.at[t, me ^ k, early]
        return remote(here, here, f_send.at[k], f_recv.at[k], place(me, 1 - t, r))

    def direct(k, x, whole):
        part = pl.ds(0, BLOCK) if whole else late
        return remote(packed.at[me ^ k, part], arrived.at[t, me, part], d_send.at[k, x], d_recv.at[k, x],
                      place(me ^ k, t ^ x, r))

    directs = [(0, 1, True), (1, 0, True), (1, 1, True)] + [(k, x, False) for k in FAR for x in (0, 1)]
    for k in FAR:
        to_owner(k).start()
    for d in directs:
        direct(*d).start()
    arrived[t, me] = packed[me]

    total = sources * BLOCK
    q = lax.broadcasted_iota(jnp.int32, (chunks * kept, 1), 0)
    q_chunk = q // kept
    q_row = q - q_chunk * kept
    q_source = q_row // slots
    target = q_source * BLOCK + q_chunk * slots + (q_row - q_source * slots)
    chooser[...] = bits(lax.broadcasted_iota(jnp.int32, (chunks * kept, total), 1) == target)

    for k in FAR:
        to_owner(k).wait_recv()
        forward(k).start()
    for d in directs:
        direct(*d).wait_recv()
    for k in FAR:
        forward(k).wait_recv()

    half_mine[...] = jnp.zeros_like(half_mine)
    half_mine[0:owners, :] = jnp.sum(
        arrived[:, :, chunks * slots : chunks * slots + owners, :].astype(jnp.float32), axis=(0, 1)
    )
    count_copy = remote(half_mine, half_other, c_send, c_recv, place(me, t, 1 - r))
    count_copy.start()

    chosen_rows = jnp.dot(
        chooser[...], arrived[...].reshape(total, CHUNK), preferred_element_type=jnp.float32
    ).astype(jnp.bfloat16)
    x = jnp.concatenate([chosen_rows[c * kept : (c + 1) * kept] for c in range(chunks)], axis=1)
    loads[2].wait()
    loads[3].wait()

    def to_group(k, n):
        here = cols.at[me, r]
        return remote(here, here, az_send.at[k, n], az_recv.at[k, n], place(me ^ k, t, r))

    def to_core(k, n):
        here = cols.at[me ^ k, r]
        return remote(here, here, ar_send.at[k, n], ar_recv.at[k, n], place(me, t, 1 - r))

    strip_width = rows.shape[3]

    def strip(core):
        return pl.ds(pl.multiple_of(core * strip_width, strip_width), strip_width)

    def to_strip(n, core):
        return remote(cols.at[me, r, n, :, strip(core)], rows.at[me, r], as_send.at[n, core], as_recv.at[me, r],
                      place(t * pieces + n, 1 - t, core))

    def strip_arrival(e, core):
        return remote(rows.at[e, core], rows.at[e, core], as_send.at[0, 0], as_recv.at[e, core], place(me, 1 - t, r))

    for n in range(pieces):
        at = slice(n * WIDTH, (n + 1) * WIDTH)
        g = jnp.dot(x, gate[:, at], preferred_element_type=jnp.float32)
        u = jnp.dot(x, up[:, at], preferred_element_type=jnp.float32)
        cols[me, r, n] = ((g / (1.0 + jnp.exp(-g))) * u).astype(jnp.bfloat16)
        for k in STEPS if n == pieces - 1 else ():
            to_group(k, 0).start()
        if n == pieces - 1:
            to_core(0, 0).start()

    for n in range(pieces):
        for core in (0, 1):
            to_strip(n, core).start()
    count_copy.wait()
    half_mine[...] = 2.0 / jnp.maximum(half_mine[...] + half_other[...], 1.0)

    in_panel = me // pieces

    def hessian(k):
        e = me ^ k
        to_core(k, 0).wait_recv()

        @pl.when(t == in_panel)
        def _():
            rows[e] = cols[e, :, me - in_panel * pieces, :, strip(r)]

        @pl.when(t != in_panel)
        def _():
            for core in (0, 1):
                strip_arrival(e, core).wait_recv()

        left = rows[e].reshape(2 * kept, strip_width)
        scale = half_mine[pl.ds(e, 1), :]
        for n in range(pieces):
            right = jnp.concatenate([cols[e, 0, n], cols[e, 1, n]], axis=0)
            h = lax.dot_general(left, right, (((0,), (0,)), ((), ())), preferred_element_type=jnp.float32)
            at = slice(n * WIDTH, (n + 1) * WIDTH)
            hess_ref[e, :, at] = h * scale[:, at]

    for n in range(pieces):
        for k in (1,) + FAR:
            if n == pieces - 1 and k == FAR[0]:
                hessian(0)
            if n == pieces - 1:
                to_group(k, 0).wait_recv()
            if n == pieces - 1:
                to_core(k, 0).start()
    for k in (1,) + FAR:
        hessian(k)

    for k in FAR:
        to_owner(k).wait_send()
        forward(k).wait_send()
    for d in directs:
        direct(*d).wait_send()
    for n in range(pieces):
        for k in STEPS:
            if n == 0:
                to_group(k, 0).wait_send()
        for k in (0,) + STEPS if n == 0 else ():
            to_core(k, 0).wait_send()
        for core in (0, 1):
            to_strip(n, core).wait_send()


def order_kernel(chosen_ref, hess_ref, out_hbm, sems):
    copies = [
        pltpu.make_async_copy(hess_ref.at[chosen_ref[s]], out_hbm.at[s], sems.at[s]) for s in range(out_hbm.shape[0])
    ]
    for copy in copies:
        copy.start()
    for copy in copies:
        copy.wait()


def fused(owners, groups, tokens, routing, chosen, gate_matrix, up_matrix):
    features, panel = gate_matrix.shape[1:]
    kept = owners * groups * ROW_CAPACITY
    chunks, pieces = features // CHUNK, panel // WIDTH
    rows_width = panel * groups // (owners * 2)
    vmem = pl.BlockSpec(memory_space=pltpu.VMEM)
    hbm = pl.BlockSpec(memory_space=pltpu.HBM)
    dma = pltpu.SemaphoreType.DMA
    hess = pl.pallas_call(
        functools.partial(hessian_kernel, owners),
        out_shape=jax.ShapeDtypeStruct((owners, rows_width, panel), jnp.float32),
        in_specs=[hbm, hbm, hbm, hbm],
        out_specs=vmem,
        scratch_shapes=[
            pltpu.VMEM(tokens.shape, jnp.bfloat16),
            pltpu.VMEM(routing.shape[::-1], jnp.int32),
            pltpu.VMEM((features, panel), jnp.bfloat16),
            pltpu.VMEM((features, panel), jnp.bfloat16),
            pltpu.VMEM((owners, BLOCK, CHUNK), jnp.bfloat16),
            pltpu.VMEM((groups, owners, BLOCK, CHUNK), jnp.bfloat16),
            pltpu.VMEM((8, panel), jnp.float32),
            pltpu.VMEM((8, panel), jnp.float32),
            pltpu.VMEM((owners, 2, pieces, kept, WIDTH), jnp.bfloat16),
            pltpu.VMEM((owners, 2, kept, rows_width), jnp.bfloat16),
            pltpu.VMEM((chunks * kept, owners * groups * BLOCK), jnp.bfloat16),
            dma((4,)),
            dma((owners,)), dma((owners,)), dma((owners,)), dma((owners,)),
            dma((owners, 2)), dma((owners, 2)),
            dma, dma,
            dma((owners, pieces)), dma((owners, pieces)), dma((owners, pieces)), dma((owners, pieces)),
            dma((pieces, 2)), dma((owners, 2)),
        ],
        compiler_params=pltpu.CompilerParams(
            collective_id=0, has_side_effects=True, vmem_limit_bytes=48 * 1024 * 1024
        ),
    )(*[pltpu.with_memory_space_constraint(a, pltpu.HBM) for a in (tokens, routing.T, gate_matrix, up_matrix)])
    out = (chosen.shape[0], rows_width, panel)
    return pl.pallas_call(
        order_kernel,
        out_shape=jax.ShapeDtypeStruct(out, jnp.float32),
        in_specs=[pl.BlockSpec(memory_space=pltpu.SMEM), vmem],
        out_specs=hbm,
        scratch_shapes=[dma((out[0],))],
        compiler_params=pltpu.CompilerParams(vmem_limit_bytes=24 * 1024 * 1024),
    )(chosen, hess)


def solution(mesh):
    owners, groups, cores = mesh.shape["exp"], mesh.shape["tp"], mesh.shape["rep"]
    small = owners == 4 and groups == 2 and cores == 2
    return jax.shard_map(
        functools.partial(fused, owners, groups) if small else local,
        mesh=mesh,
        in_specs=(
            P(("grp", "exp", "tp", "rep"), None),
            P(("grp", "exp", "tp", "rep"), None),
            P("grp"),
            P("exp", None, "tp"),
            P("exp", None, "tp"),
        ),
        out_specs=P("grp", ("exp", "rep"), "tp"),
        check_vma=False,
    )
```
